512 devices in a mesh: expert: 128 (over z, y, core), dp: 4 (over x).
Axes of the slice: x: 4, y: 8, z: 8, core: 2. Of those that a mesh axis runs over, the one named last changes fastest.
Arguments:
- tokens: bfloat16 [65536, 7168], P(('expert', 'dp')), may hold values from -6 to 6
- expert_ids: int32 [65536, 8], P(('expert', 'dp')), may hold values from 0 to 255, all different within a row; in each aligned block of 128 rows (0 to 127, 128 to 255, ...) at most 8 rows name the same one
- weight_cols: bfloat16 [256, 1024, 640], P('expert', 'dp'), may hold values from -12 to 12
- uinv_panel: float32 [256, 128, 128], P('expert'), as said below
- u_window: float32 [256, 128, 512], P('expert'), may hold values from -0.5 to 0.5
- panel_index: int32 [1], replicated, may hold values from 0 to 51
Outputs:
- q_panel: bfloat16 [256, 1024, 128], P('expert', 'dp')
- w_window: bfloat16 [256, 1024, 512], P('expert', 'dp')
- hess_grad: float32 [256, 1024, 640], P('expert', 'dp')
The draws below stay inside these ranges and needn't reach their ends.
Inputs may be any that keep to these rules, and one draw needn't show every extreme that they name: `expert_ids`: each row names 8 different experts; within the rows of one device no expert is named by more than 8 rows, a bound that the rows of some device reach; every expert is named by some row. `uinv_panel`: each block is upper triangular, with diagonal entries from 1 to 3.
All inputs are finite; a program needn't handle non-finite values.
Results may differ from the reference program's by a relative error of at most 0.013.
Values may be sent and summed in bfloat16 or wider, within the bound.
A program may use at most 64 MiB of HBM per device.

```python
import math
import jax
import jax.numpy as jnp
import numpy as np
from jax import lax

D = 7168
TOP = 8
OUT_ROWS = 1024
PANEL = 128
WIN = 512
TOK_DEV = 128
EXPERTS = 256
MOST = 8
COLS = 640
TOKENS = 65536
N_EXPERT = 128
N_DP = 4


def draw_uinv_panel(key, part):
    key = jax.random.fold_in(key, 7)
    diag_key, upper_key = jax.random.split(key)
    diagonal = jax.random.uniform(diag_key, (EXPERTS, PANEL), jnp.float32, 1.0, 3.0)
    spread = jax.random.normal(upper_key, (EXPERTS, PANEL, PANEL), jnp.float32) * (0.6 / math.sqrt(PANEL))
    upper_part = jnp.triu(spread, 1)
    identity = jnp.eye(PANEL, dtype=jnp.float32)
    return upper_part + diagonal[:, :, None] * identity[None, :, :]


def shard_levels(own_key, extent, pieces, low, high):
    def one(axis_at, parts):
        draws = jax.random.uniform(jax.random.fold_in(jax.random.fold_in(own_key, 6), axis_at), (parts,), jnp.float32, low / len(pieces), high / len(pieces))
        return jnp.repeat(jnp.exp(draws), extent[axis_at] // parts).reshape((-1,) + (1,) * (len(extent) - axis_at - 1))

    level = one(*pieces[0])
    for cut in pieces[1:]:
        level = level * one(*cut)
    return level


def shared_out(rng, own, number, rows, number_of, top, reach, slope):
    sequence = jax.random.permutation(rng, number_of)
    heavy_load, ordinary = shares(number_of, rows * top, reach, slope, True), shares(number_of, rows * top, reach, slope, False)
    places = jnp.arange(number_of)

    def named(lengths, turn):
        used = int((lengths > 0).sum())
        fixed = max(1, used // 4)
        passed = fixed + (places - fixed + turn * (used - fixed)) % max(1, number_of - fixed)
        return jnp.zeros((number_of,), jnp.int32).at[sequence[jnp.where(places < fixed, places, passed)]].set(jnp.asarray(lengths, jnp.int32))

    lengths = jnp.where(number % 4 == 0, named(heavy_load, number // 4), named(ordinary, number - number // 4 - 1))
    mixed = jax.random.permutation(jax.random.fold_in(own, 3), number_of)
    source_of, receiver = mixed[0:number_of // 2 * 2:2], mixed[1:number_of // 2 * 2:2]
    room = jnp.minimum(lengths[source_of] - 1, reach - lengths[receiver]) // 2
    room = jnp.where((source_of == sequence[0]) | (receiver == sequence[0]) | (lengths[receiver] == 0), 0, jnp.maximum(room, 0))
    passed = jax.random.randint(jax.random.fold_in(own, 4), (number_of // 2,), 0, 1 << 20) % (room + 1)
    lengths = lengths.at[source_of].add(-passed).at[receiver].add(passed)
    labels = jnp.searchsorted(jnp.cumsum(lengths), jnp.arange(rows * top), side="right").astype(jnp.int32)
    listing = labels.reshape(top, rows).T
    listing = listing[jax.random.permutation(jax.random.fold_in(own, 1), rows)]
    turn = jax.random.randint(jax.random.fold_in(own, 2), (rows, 1), 0, top)
    return jnp.take_along_axis(listing, (jnp.arange(top)[None, :] + turn) % top, axis=1)


def shares(count, total, reach, slope, full):
    portions = [(1 << 20) // math.isqrt(rank ** slope) + 1 for rank in range(1, count + 1)]
    largest = reach if full else min(reach, max(-(-total // count), total * portions[0] // sum(portions)))
    least = 1 if total - largest >= count - 1 else 0
    holding, spare = [largest] + [least] * (count - 1), total - largest - least * (count - 1)
    while spare > 0:
        movable = [i for i in range(1, count) if holding[i] < largest] or [i for i in range(1, count) if holding[i] < reach]
        mass, budget = sum([portions[i] for i in movable]), spare
        for i in movable:
            more = min(reach - holding[i], max(1, budget * portions[i] // mass), spare)
            holding[i] = holding[i] + more
            spare = spare - more
    return np.array(holding)


def scatter_about(own_key, dims, width, reach, shards=(), held_as=jnp.bfloat16):
    drawn = width * jax.random.normal(own_key, dims, jnp.float32)
    if shards:
        drawn = drawn * shard_levels(own_key, dims, shards, -0.22, 0.18)
    return jnp.clip(drawn, -reach, reach).astype(held_as)


def setup_inputs(seed: int = 0) -> dict:
    streams_of = jax.random.split(jax.random.key(seed), 7)
    tokens = scatter_about(streams_of[0], (TOKENS, D), 1.0, 6.0, ((0, 512),))
    expert_ids_keys = jax.random.split(jax.random.fold_in(streams_of[1], 1), TOKENS // TOK_DEV)
    expert_ids_turns = jax.random.permutation(jax.random.fold_in(streams_of[1], 3), TOKENS // TOK_DEV)
    expert_ids = jax.vmap(lambda own, number: shared_out(jax.random.fold_in(streams_of[1], 2), own, number, TOK_DEV, EXPERTS, TOP, MOST, 2))(expert_ids_keys, expert_ids_turns).reshape((TOKENS, TOP))
    weight_cols = scatter_about(streams_of[2], (EXPERTS, OUT_ROWS, COLS), 2.0, 12.0, ((0, 128), (1, 4)))
    uinv_panel = draw_uinv_panel(jax.random.fold_in(streams_of[6], 71), 0)
    u_window = scatter_about(streams_of[4], (EXPERTS, PANEL, WIN), PANEL ** -0.5, 0.5, ((0, 128),), jnp.float32)
    panel_index = jax.random.randint(streams_of[5], (1,), 0, D // PANEL - WIN // PANEL).astype(jnp.int32)
    return {"tokens": tokens, "expert_ids": expert_ids, "weight_cols": weight_cols, "uinv_panel": uinv_panel, "u_window": u_window, "panel_index": panel_index}


TWO_PI = 2.0 * math.pi


def quantize_step(weights, uinv_block, upper_block, hessian):
    panel_cols = weights[:, :PANEL]
    row_scale = (jnp.max(jnp.abs(panel_cols), axis=1, keepdims=True) + 1e-6) / 7.0
    scaled = panel_cols / row_scale
    quantized = row_scale * (scaled - jnp.sin(TWO_PI * scaled) / TWO_PI)
    quant_error = panel_cols - quantized
    left_part = jnp.dot(quant_error, uinv_block, precision=lax.Precision.HIGHEST)
    correction = jnp.dot(left_part, upper_block, precision=lax.Precision.HIGHEST)
    change_all = jnp.concatenate([-quant_error, -correction], axis=1)
    hess_grad = jnp.dot(change_all, hessian, precision=lax.Precision.HIGHEST)
    return quantized.astype(jnp.bfloat16), (weights[:, PANEL:] - correction).astype(jnp.bfloat16), hess_grad


def reference(tokens, expert_ids, weight_cols, uinv_panel, u_window, panel_index):
    first_col = (panel_index[0] * PANEL).astype(jnp.int32)
    window = lax.dynamic_slice_in_dim(tokens, first_col, PANEL + WIN, 1)
    flat_ids = expert_ids.reshape(-1).astype(jnp.int32)
    sorted_pairs = jnp.argsort(flat_ids, stable=True).astype(jnp.int32)
    row_cap = MOST * N_EXPERT * N_DP
    token_of = jnp.concatenate([sorted_pairs // TOP, jnp.zeros((row_cap,), jnp.int32)]).astype(jnp.int32)
    counts = jnp.zeros((EXPERTS,), jnp.int32).at[flat_ids].add(1)
    offsets = (jnp.cumsum(counts) - counts).astype(jnp.int32)

    def one_expert(expert):
        token_index = lax.dynamic_slice_in_dim(token_of, offsets[expert], row_cap)
        slot_live = jnp.arange(row_cap, dtype=jnp.int32) < counts[expert]
        routed_rows = jnp.where(slot_live[:, None], window[token_index].astype(jnp.float32), jnp.zeros((), jnp.float32))
        gram_sum = jnp.dot(routed_rows.T, routed_rows, precision=lax.Precision.HIGHEST, preferred_element_type=jnp.float32)
        hessian = gram_sum / counts[expert].astype(jnp.float32)
        return quantize_step(weight_cols[expert].astype(jnp.float32), uinv_panel[expert], u_window[expert], hessian)

    q_panel, w_window, hess_grad = lax.map(one_expert, jnp.arange(EXPERTS, dtype=jnp.int32))
    return q_panel, w_window, hess_grad
```

```python
import functools
import math

import jax
import jax.numpy as jnp
from jax import lax
from jax.experimental import pallas as pl
from jax.experimental.pallas import tpu as pltpu
from jax.sharding import PartitionSpec as P

PANEL = 128
SLOTS = 8
TWO_PI = 2.0 * math.pi
HIGHEST = lax.Precision.HIGHEST
MESH = pl.DeviceIdType.MESH
F32 = jnp.float32
BF16 = jnp.bfloat16


def sin_turn(turns):
    part = turns - jnp.round(turns)
    half = jnp.where(part < 0, -0.5, 0.5)
    part = jnp.where(jnp.abs(part) > 0.25, half - part, part)
    angle = part * TWO_PI
    square = angle * angle
    series = jnp.full_like(square, -1.0 / math.factorial(11))
    for power in (9, 7, 5, 3, 1):
        sign = 1.0 if power % 4 == 1 else -1.0
        series = series * square + sign / math.factorial(power)
    return angle * series


def kernel(
    line, n_dp,
    win_ref, ids_ref, w_ref, uinv_ref, uw_ref,
    q_ref, ww_ref, hg_ref,
    tok, idb, outb, inb, cnt_out, cnt_in, change, gram_out, gram_in, whole, hess,
    tok_s, tok_r, ids_s, ids_r, row_s, row_r, cnt_s, cnt_r, rs_s, rs_r, ag_s, ag_r,
):
    idx = lax.axis_index("expert")
    xpos = lax.axis_index("dp")
    core = idx % 2
    y = (idx // 2) % line
    z = idx // (2 * line)
    dests = 2 * line
    pairs = line // 2
    blocks = w_ref.shape[2] // PANEL
    upper = [(b, c) for b in range(blocks) for c in range(b, blocks)]
    part_rows = PANEL // n_dp
    body = len(upper) * part_rows
    tokens = win_ref.shape[0]

    stride1 = 2 * line - (2 * line - 2) * core
    place1 = z * (1 - core) + y * core
    base1 = idx - place1 * stride1
    stride2 = 2 + (2 * line - 2) * core
    place2 = y * (1 - core) + z * core
    base2 = idx - core - place2 * stride2
    self_dest = 2 * place2 + core
    my_slot = core * line + place2

    barrier = pltpu.get_barrier_semaphore()

    def greet(device, at=xpos):
        pl.semaphore_signal(barrier, inc=1, device_id=(device, at), device_id_type=MESH)

    @pl.loop(1, line)
    def _(d):
        greet(base1 + ((place1 + d) % line) * stride1)

    @pl.loop(1, line)
    def _(d):
        greet(base2 + ((place2 + d) % line) * stride2 + core)

    @pl.loop(0, line)
    def _(d):
        other = 1 - core
        stride = 2 + (2 * line - 2) * other
        place = y * (1 - other) + z * other
        greet(idx - core - place * stride + d * stride + other)

    @pl.loop(1, n_dp)
    def _(d):
        greet(idx, (xpos + d) % n_dp)

    pl.semaphore_wait(barrier, 3 * line - 2 + n_dp - 1)

    @pl.loop(1, line)
    def _(d):
        peer = (base1 + ((place1 + d) % line) * stride1, xpos)
        pltpu.make_async_remote_copy(
            ids_ref, idb.at[place1], ids_s, ids_r.at[place1], device_id=peer, device_id_type=MESH
        ).start()
        pltpu.make_async_remote_copy(
            win_ref, tok.at[place1], tok_s, tok_r.at[place1], device_id=peer, device_id_type=MESH
        ).start()

    tok[place1] = win_ref[...]
    idb[place1] = ids_ref[...]

    for i in range(2):
        panel = w_ref[i, :, :PANEL].astype(F32)
        scale = (jnp.max(jnp.abs(panel), axis=1, keepdims=True) + 1e-6) / 7.0
        error = scale * sin_turn(panel / scale) * (1.0 / TWO_PI)
        q_ref[i] = (panel - error).astype(BF16)
        change[i, :, :PANEL] = (-error).astype(BF16)
        left = jnp.dot(error, uinv_ref[i], precision=HIGHEST, preferred_element_type=F32)
        correction = jnp.dot(left, uw_ref[i], precision=HIGHEST, preferred_element_type=F32)
        ww_ref[i] = (w_ref[i, :, PANEL:].astype(F32) - correction).astype(BF16)
        change[i, :, PANEL:] = (-correction).astype(BF16)

    row = lax.broadcasted_iota(jnp.int32, (2 * dests, 2 * tokens), 0)
    named = (
        (row // 4) * (4 + (4 * line - 4) * core)
        + row % 4
        + (1 - core) * z * (4 * line)
        + core * y * 4
    )
    before = (
        lax.broadcasted_iota(jnp.int32, (2 * tokens, 2 * tokens), 0)
        < lax.broadcasted_iota(jnp.int32, (2 * tokens, 2 * tokens), 1)
    ).astype(F32).astype(BF16)
    slot = lax.broadcasted_iota(jnp.int32, (2 * SLOTS, 2 * tokens), 0).astype(F32)
    cnt_out[...] = jnp.zeros_like(cnt_out)

    def send_rows(i, k, q):
        d = (self_dest + k) % dests
        peer = (base2 + (d // 2) * stride2 + d % 2, xpos)
        if q is None:
            src, dst = outb.at[i, d], inb.at[i, my_slot]
        else:
            src, dst = outb.at[i, d, q], inb.at[i, my_slot, q]
        pltpu.make_async_remote_copy(
            src, dst, row_s.at[i], row_r.at[i], device_id=peer, device_id_type=MESH
        ).start()

    @pl.loop(0, pairs)
    def _(t):
        q = (place1 // 2 + t) % pairs
        for s in range(2):
            j = 2 * q + s

            @pl.when(j != place1)
            def _():
                pltpu.make_async_copy(ids_ref, idb.at[j], ids_r.at[j]).wait()
                pltpu.make_async_copy(win_ref, tok.at[j], tok_r.at[j]).wait()

        ids = jnp.concatenate([idb[2 * q], idb[2 * q + 1]], axis=1)
        member = jnp.zeros(named.shape, F32)
        for k in range(ids.shape[0]):
            member = member + jnp.where(ids[k : k + 1, :] == named, 1.0, 0.0)
        rank = jnp.dot(member.astype(BF16), before, preferred_element_type=F32)
        rank = jnp.where(member > 0.5, rank, -1.0)
        half = member[:, :tokens] + member[:, tokens:]
        cnt_out[...] += jnp.broadcast_to(half[:, None, :], cnt_out.shape)
        source = tok[pl.ds(2 * q, 2)].reshape(2 * tokens, win_ref.shape[1])
        step = min(8, 2 * dests)
        for e in range(0, 2 * dests, step):
            pick = jnp.where(rank[e : e + step, None, :] == slot[None], 1.0, 0.0)
            pick = pick.reshape(step * 2 * SLOTS, 2 * tokens).astype(BF16)
            rows = jnp.dot(pick, source, preferred_element_type=F32).astype(BF16)
            rows = rows.reshape(step, 2 * SLOTS, -1)
            for m in range(step):
                outb[(e + m) % 2, (e + m) // 2, q] = rows[m]
        inb[0, my_slot, q] = outb[0, self_dest, q]
        inb[1, my_slot, q] = outb[1, self_dest, q]

        @pl.loop(1, dests)
        def _(k):
            send_rows(0, k, q)

    @pl.loop(1, dests)
    def _(k):
        d = (self_dest + k) % dests
        peer = (base2 + (d // 2) * stride2 + d % 2, xpos)
        pltpu.make_async_remote_copy(
            cnt_out.at[pl.ds(2 * d, 2)], cnt_in.at[my_slot], cnt_s, cnt_r,
            device_id=peer, device_id_type=MESH,
        ).start()
        send_rows(1, k, None)

    cnt_in[my_slot] = cnt_out[pl.ds(2 * self_dest, 2)]

    def rows_wait(i):
        view = inb.at[i, pl.ds(0, dests - 1)]
        pltpu.make_async_copy(view, view, row_r.at[i]).wait()

    def gram(i):
        rows_wait(i)
        held = inb.at[i]
        rows = held[...].reshape(-1, w_ref.shape[2])
        for b in range(blocks):
            product = lax.dot_general(
                rows[:, b * PANEL : (b + 1) * PANEL], rows[:, b * PANEL :],
                (((0,), (0,)), ((), ())), preferred_element_type=F32,
            ).astype(BF16)
            for c in range(b, blocks):
                t = upper.index((b, c))
                for p in range(n_dp):
                    gram_out[i, p, t * part_rows : (t + 1) * part_rows, :] = product[
                        p * part_rows : (p + 1) * part_rows,
                        (c - b) * PANEL : (c - b + 1) * PANEL,
                    ]
        count = jnp.sum(cnt_in[:, i], axis=0)[:1]
        count = jnp.broadcast_to(count, (16, PANEL)).astype(BF16)
        for p in range(n_dp):
            gram_out[i, p, body:, :] = count
        for d in range(1, n_dp):
            other = (xpos + d) % n_dp
            pltpu.make_async_remote_copy(
                gram_out.at[i, other], gram_in.at[i, d - 1], rs_s.at[i, d - 1], rs_r.at[i, d - 1],
                device_id=(idx, other), device_id_type=MESH,
            ).start()

    def share(i):
        for d in range(1, n_dp):
            pltpu.make_async_copy(gram_in.at[i, d - 1], gram_in.at[i, d - 1], rs_r.at[i, d - 1]).wait()
        total = gram_out[i, xpos].astype(F32)
        for d in range(1, n_dp):
            total = total + gram_in[i, d - 1].astype(F32)
        whole[i, xpos] = total[:body].astype(BF16)
        for d in range(1, n_dp):
            other = (xpos + d) % n_dp
            pltpu.make_async_remote_copy(
                whole.at[i, xpos], whole.at[i, xpos], ag_s.at[i, d - 1], ag_r.at[i, xpos],
                device_id=(idx, other), device_id_type=MESH,
            ).start()
        return 1.0 / jnp.sum(total[body : body + 1], axis=1, keepdims=True)

    def finish(i, inverse):
        for d in range(1, n_dp):
            other = (xpos + d) % n_dp
            pltpu.make_async_copy(whole.at[i, other], whole.at[i, other], ag_r.at[i, other]).wait()
        for t, (b, c) in enumerate(upper):
            for p in range(n_dp):
                hess[b * PANEL + p * part_rows : b * PANEL + (p + 1) * part_rows,
                     c * PANEL : (c + 1) * PANEL] = whole[i, p, t * part_rows : (t + 1) * part_rows, :]
        for c in range(blocks):
            low, high = c * PANEL, (c + 1) * PANEL
            out = jnp.dot(change[i, :, :high], hess[:high, low:high], preferred_element_type=F32)
            if high < w_ref.shape[2]:
                out = out + lax.dot_general(
                    change[i, :, high:], hess[low:high, high:],
                    (((1,), (1,)), ((), ())), preferred_element_type=F32,
                )
            hg_ref[i, :, low:high] = out * inverse

    pltpu.make_async_copy(cnt_in.at[pl.ds(0, dests - 1)], cnt_in.at[pl.ds(0, dests - 1)], cnt_r).wait()
    gram(0)
    inverse0 = share(0)
    finish(0, inverse0)
    gram(1)
    inverse1 = share(1)
    finish(1, inverse1)

    for i in range(2):
        view = outb.at[i, pl.ds(0, dests - 1)]
        pltpu.make_async_copy(view, view, row_s.at[i]).wait()
        for d in range(n_dp - 1):
            pltpu.make_async_copy(gram_in.at[i, d], gram_in.at[i, d], rs_s.at[i, d]).wait()
            pltpu.make_async_copy(whole.at[i, 0], whole.at[i, 0], ag_s.at[i, d]).wait()
    view = cnt_in.at[pl.ds(0, dests - 1)]
    pltpu.make_async_copy(view, view, cnt_s).wait()
    view = tok.at[pl.ds(0, line - 1)]
    pltpu.make_async_copy(view, view, tok_s).wait()
    view = idb.at[pl.ds(0, line - 1)]
    pltpu.make_async_copy(view, view, ids_s).wait()


def per_device(tokens, expert_ids, weight_cols, uinv_panel, u_window, panel_index):
    n_expert, n_dp = lax.axis_size("expert"), lax.axis_size("dp")
    line = math.isqrt(n_expert // 2)
    dests = 2 * line
    rows, columns = weight_cols.shape[1:]
    n_tok, top_k = expert_ids.shape
    window = lax.dynamic_slice_in_dim(tokens, panel_index[0] * PANEL, columns, 1)
    blocks = columns // PANEL
    body = blocks * (blocks + 1) // 2 * (PANEL // n_dp)
    dma = pltpu.SemaphoreType.DMA
    vmem = pl.BlockSpec(memory_space=pltpu.VMEM)
    return pl.pallas_call(
        functools.partial(kernel, line, n_dp),
        out_shape=(
            jax.ShapeDtypeStruct((2, rows, PANEL), BF16),
            jax.ShapeDtypeStruct((2, rows, columns - PANEL), BF16),
            jax.ShapeDtypeStruct((2, rows, columns), F32),
        ),
        in_specs=[vmem] * 5,
        out_specs=(vmem,) * 3,
        scratch_shapes=[
            pltpu.VMEM((line, n_tok, columns), BF16),
            pltpu.VMEM((line, top_k, n_tok), jnp.int32),
            pltpu.VMEM((2, dests, line // 2, 2 * SLOTS, columns), BF16),
            pltpu.VMEM((2, dests, line // 2, 2 * SLOTS, columns), BF16),
            pltpu.VMEM((2 * dests, 8, n_tok), F32),
            pltpu.VMEM((dests, 2, 8, n_tok), F32),
            pltpu.VMEM((2, rows, columns), BF16),
            pltpu.VMEM((2, n_dp, body + 16, PANEL), BF16),
            pltpu.VMEM((2, n_dp - 1, body + 16, PANEL), BF16),
            pltpu.VMEM((2, n_dp, body, PANEL), BF16),
            pltpu.VMEM((columns, columns), BF16),
            dma, dma((line,)), dma, dma((line,)), dma((2,)), dma((2,)), dma, dma,
            dma((2, n_dp - 1)), dma((2, n_dp - 1)), dma((2, n_dp - 1)), dma((2, n_dp)),
        ],
        compiler_params=pltpu.CompilerParams(
            collective_id=0, has_side_effects=True, vmem_limit_bytes=56 * 1024 * 1024
        ),
    )(window, expert_ids.T, weight_cols, uinv_panel, u_window)


def solution(mesh):
    placed = (
        P(("expert", "dp"), None),
        P(("expert", "dp"), None),
        P("expert", "dp", None),
        P("expert", None, None),
        P("expert", None, None),
        P(),
    )
    return jax.shard_map(
        per_device,
        mesh=mesh,
        in_specs=placed,
        out_specs=(P("expert", "dp", None), P("expert", "dp", None), P("expert", "dp", None)),
        check_vma=False,
    )
```

```python
import functools
import math

import jax
import jax.numpy as jnp
from jax import lax
from jax.experimental import pallas as pl
from jax.experimental.pallas import tpu as pltpu
from jax.sharding import PartitionSpec as P

PANEL = 128
SLOTS = 8
TWO_PI = 2.0 * math.pi
HIGHEST = lax.Precision.HIGHEST
MESH = pl.DeviceIdType.MESH
F32 = jnp.float32
BF16 = jnp.bfloat16


def sin_turn(turns):
    part = turns - jnp.round(turns)
    half = jnp.where(part < 0, -0.5, 0.5)
    part = jnp.where(jnp.abs(part) > 0.25, half - part, part)
    angle = part * TWO_PI
    square = angle * angle
    series = jnp.full_like(square, -1.0 / math.factorial(11))
    for power in (9, 7, 5, 3, 1):
        sign = 1.0 if power % 4 == 1 else -1.0
        series = series * square + sign / math.factorial(power)
    return angle * series


def upper_tiles(blocks):
    return [(b, c) for b in range(blocks) for c in range(b, blocks)]


def route_kernel(
    line, n_dp,
    win_ref, ids_ref, w_hbm, uinv_hbm, uw_hbm,
    change, whole, total_cnt,
    w_ref, uinv_ref, uw_ref, tok, idb, outb, inb, cnt_out, cnt_in, gram_out, gram_in,
    load_s, tok_s, tok_r, ids_s, ids_r, row_s, row_r, cnt_s, cnt_r, rs_s, rs_r, ag_s, ag_r,
):
    idx = lax.axis_index("expert")
    xpos = lax.axis_index("dp")
    core = idx % 2
    y = (idx // 2) % line
    z = idx // (2 * line)
    dests = 2 * line
    pairs = line // 2
    columns = w_ref.shape[2]
    blocks = columns // PANEL
    upper = upper_tiles(blocks)
    part_rows = PANEL // n_dp
    body = len(upper) * part_rows
    tokens = tok.shape[1]
    own = line - 2

    loads = [
        pltpu.make_async_copy(w_hbm, w_ref, load_s.at[0]),
        pltpu.make_async_copy(uinv_hbm, uinv_ref, load_s.at[1]),
        pltpu.make_async_copy(uw_hbm, uw_ref, load_s.at[2]),
    ]
    for load in loads:
        load.start()

    stride1 = 2 * line - (2 * line - 2) * core
    place1 = z * (1 - core) + y * core
    base1 = idx - place1 * stride1
    stride2 = 2 + (2 * line - 2) * core
    place2 = y * (1 - core) + z * core
    base2 = idx - core - place2 * stride2
    self_dest = 2 * place2 + core
    my_slot = core * line + place2

    barrier = pltpu.get_barrier_semaphore()

    def greet(device, at=xpos):
        pl.semaphore_signal(barrier, inc=1, device_id=(device, at), device_id_type=MESH)

    @pl.loop(1, line)
    def _(d):
        greet(base1 + ((place1 + d) % line) * stride1)

    @pl.loop(1, line)
    def _(d):
        greet(base2 + ((place2 + d) % line) * stride2 + core)

    @pl.loop(0, line)
    def _(d):
        other = 1 - core
        stride = 2 + (2 * line - 2) * other
        place = y * (1 - other) + z * other
        greet(idx - core - place * stride + d * stride + other)

    @pl.loop(1, n_dp)
    def _(d):
        greet(idx, (xpos + d) % n_dp)

    tok[own] = win_ref[...]
    idb[own] = ids_ref[...]

    pl.semaphore_wait(barrier, 3 * line - 2 + n_dp - 1)

    right = (base1 + ((place1 + 1) % line) * stride1, xpos)
    left = (base1 + ((place1 + line - 1) % line) * stride1, xpos)

    for step in range(1, pairs + 1):
        for way in range(1 if step == pairs else 2):
            slot = 2 * (step - 1) + way + (1 if step == pairs else 0)
            at = (place1 + (step if way == 0 else line - step)) % line
            pltpu.make_async_remote_copy(
                ids_ref, idb.at[slot], ids_s, ids_r.at[slot],
                device_id=(base1 + at * stride1, xpos), device_id_type=MESH,
            ).start()

    def hop(source, target, way, far):
        rows = pl.ds(way * (tokens // 2), tokens // 2) if far else pl.ds(0, tokens)
        sem = 2 * pairs - 2 + way if far else target
        return pltpu.make_async_remote_copy(
            tok.at[source, rows], tok.at[target, rows], tok_s.at[sem], tok_r.at[sem],
            device_id=right if way == 0 else left, device_id_type=MESH,
        )

    hops = []

    def start_hops(step):
        for way in range(2):
            far = step == pairs
            source = own if step == 1 else 2 * (step - 2) + way
            copy = hop(source, line - 1 if far else 2 * (step - 1) + way, way, far)
            copy.start()
            hops.append(copy)

    start_hops(1)

    def weights(i):
        panel = w_ref[i, :, :PANEL].astype(F32)
        scale = (jnp.max(jnp.abs(panel), axis=1, keepdims=True) + 1e-6) / 7.0
        error = scale * sin_turn(panel / scale) * (1.0 / TWO_PI)
        change[i, :, :PANEL] = (-error).astype(BF16)
        left_part = jnp.dot(error, uinv_ref[i], precision=HIGHEST, preferred_element_type=F32)
        correction = jnp.dot(left_part, uw_ref[i], precision=HIGHEST, preferred_element_type=F32)
        change[i, :, PANEL:] = (-correction).astype(BF16)

    row = lax.broadcasted_iota(jnp.int32, (2 * dests, 2 * tokens), 0)
    named = (
        (row // 4) * (4 + (4 * line - 4) * core)
        + row % 4
        + (1 - core) * z * (4 * line)
        + core * y * 4
    )
    before = (
        lax.broadcasted_iota(jnp.int32, (2 * tokens, 2 * tokens), 0)
        < lax.broadcasted_iota(jnp.int32, (2 * tokens, 2 * tokens), 1)
    ).astype(F32).astype(BF16)
    slot_of = lax.broadcasted_iota(jnp.int32, (2 * SLOTS, 2 * tokens), 0).astype(F32)
    cnt_out[...] = jnp.zeros_like(cnt_out)

    def send_rows(i, k, q):
        d = (self_dest + k) % dests
        peer = (base2 + (d // 2) * stride2 + d % 2, xpos)
        if q is None:
            src, dst = outb.at[i, d], inb.at[i, my_slot]
        else:
            src, dst = outb.at[i, d, q], inb.at[i, my_slot, q]
        pltpu.make_async_remote_copy(
            src, dst, row_s.at[i], row_r.at[i], device_id=peer, device_id_type=MESH
        ).start()

    def pick_rows(q):
        ids = jnp.concatenate([idb[2 * q], idb[2 * q + 1]], axis=1)
        member = jnp.zeros(named.shape, F32)
        for k in range(ids.shape[0]):
            member = member + jnp.where(ids[k : k + 1, :] == named, 1.0, 0.0)
        rank = jnp.dot(member.astype(BF16), before, preferred_element_type=F32)
        rank = jnp.where(member > 0.5, rank, -1.0)
        half = member[:, :tokens] + member[:, tokens:]
        cnt_out[...] += jnp.broadcast_to(half[:, None, :], cnt_out.shape)
        source = tok[pl.ds(2 * q, 2)].reshape(2 * tokens, columns)
        step = min(8, 2 * dests)
        for e in range(0, 2 * dests, step):
            pick = jnp.where(rank[e : e + step, None, :] == slot_of[None], 1.0, 0.0)
            pick = pick.reshape(step * 2 * SLOTS, 2 * tokens).astype(BF16)
            rows = jnp.dot(pick, source, preferred_element_type=F32).astype(BF16)
            rows = rows.reshape(step, 2 * SLOTS, -1)
            for m in range(step):
                outb[(e + m) % 2, (e + m) // 2, q] = rows[m]
        inb[0, my_slot, q] = outb[0, self_dest, q]
        inb[1, my_slot, q] = outb[1, self_dest, q]

        @pl.loop(1, dests)
        def _(k):
            send_rows(0, k, q)

    for load in loads:
        load.wait()
    weights(0)
    for q in range(pairs):
        last = q == pairs - 1
        for way in range(2):
            source = 2 * q + way
            if not last or way == 1:
                pltpu.make_async_copy(ids_ref, idb.at[source], ids_r.at[source]).wait()
            if not last:
                pltpu.make_async_copy(tok.at[source], tok.at[source], tok_r.at[source]).wait()
            else:
                half = tok.at[line - 1, pl.ds(way * (tokens // 2), tokens // 2)]
                pltpu.make_async_copy(half, half, tok_r.at[source]).wait()
        if not last:
            start_hops(q + 2)
        pick_rows(q)
        if q == 0:
            weights(1)

    @pl.loop(1, dests)
    def _(k):
        d = (self_dest + k) % dests
        peer = (base2 + (d // 2) * stride2 + d % 2, xpos)
        pltpu.make_async_remote_copy(
            cnt_out.at[pl.ds(2 * d, 2)], cnt_in.at[my_slot], cnt_s, cnt_r,
            device_id=peer, device_id_type=MESH,
        ).start()


    @pl.loop(1, dests)
    def _(k):
        send_rows(1, k, None)

    cnt_in[my_slot] = cnt_out[pl.ds(2 * self_dest, 2)]

    def sent(i):
        return pl.ds(0, body + 16 * i)

    def gram(i):
        view = inb.at[i, pl.ds(0, dests - 1)]
        pltpu.make_async_copy(view, view, row_r.at[i]).wait()
        held = inb.at[i]
        rows = held[...].reshape(-1, columns)
        for b in range(blocks):
            product = lax.dot_general(
                rows[:, b * PANEL : (b + 1) * PANEL], rows[:, b * PANEL :],
                (((0,), (0,)), ((), ())), preferred_element_type=F32,
            ).astype(BF16)
            for c in range(b, blocks):
                t = upper.index((b, c))
                for p in range(n_dp):
                    gram_out[i, p, t * part_rows : (t + 1) * part_rows, :] = product[
                        p * part_rows : (p + 1) * part_rows,
                        (c - b) * PANEL : (c - b + 1) * PANEL,
                    ]
        if i == 1:
            view = cnt_in.at[pl.ds(0, dests - 1)]
            pltpu.make_async_copy(view, view, cnt_r).wait()
            count = jnp.sum(cnt_in[...], axis=0).reshape(16, PANEL).astype(BF16)
            for p in range(n_dp):
                gram_out[i, p, body:, :] = count
        for d in range(1, n_dp):
            other = (xpos + d) % n_dp
            pltpu.make_async_remote_copy(
                gram_out.at[i, other, sent(i)], gram_in.at[i, d - 1, sent(i)], rs_s.at[i, d - 1], rs_r.at[i, d - 1],
                device_id=(idx, other), device_id_type=MESH,
            ).start()

    def share(i):
        for d in range(1, n_dp):
            view = gram_in.at[i, d - 1, sent(i)]
            pltpu.make_async_copy(view, view, rs_r.at[i, d - 1]).wait()
        total = gram_out[i, xpos, sent(i)].astype(F32)
        for d in range(1, n_dp):
            total = total + gram_in[i, d - 1, sent(i)].astype(F32)
        whole[i, xpos] = total[:body].astype(BF16)
        for d in range(1, n_dp):
            other = (xpos + d) % n_dp
            pltpu.make_async_remote_copy(
                whole.at[i, xpos], whole.at[i, xpos], ag_s.at[i, d - 1], ag_r.at[i, xpos],
                device_id=(idx, other), device_id_type=MESH,
            ).start()
        if i == 1:
            total_cnt[...] = total[body:].reshape(2, 8, PANEL)

    def gathered(i):
        for d in range(1, n_dp):
            other = (xpos + d) % n_dp
            pltpu.make_async_copy(whole.at[i, other], whole.at[i, other], ag_r.at[i, other]).wait()

    gram(0)
    share(0)
    gram(1)
    share(1)
    gathered(0)
    gathered(1)

    for i in range(2):
        view = outb.at[i, pl.ds(0, dests - 1)]
        pltpu.make_async_copy(view, view, row_s.at[i]).wait()
        for d in range(n_dp - 1):
            view = gram_in.at[i, d, sent(i)]
            pltpu.make_async_copy(view, view, rs_s.at[i, d]).wait()
            pltpu.make_async_copy(whole.at[i, 0], whole.at[i, 0], ag_s.at[i, d]).wait()
    view = cnt_in.at[pl.ds(0, dests - 1)]
    pltpu.make_async_copy(view, view, cnt_s).wait()
    for copy in hops:
        copy.wait_send()
    view = idb.at[pl.ds(0, line - 1)]
    pltpu.make_async_copy(view, view, ids_s).wait()


def last_kernel(n_dp, w_ref, change, whole, cnt, q_ref, ww_ref, hg_ref, hess):
    columns = w_ref.shape[2]
    blocks = columns // PANEL
    part_rows = PANEL // n_dp
    weights = w_ref[0].astype(F32) + change[0].astype(F32)
    q_ref[0] = weights[:, :PANEL].astype(BF16)
    ww_ref[0] = weights[:, PANEL:].astype(BF16)
    inverse = 1.0 / jnp.sum(cnt[0, :1], axis=1, keepdims=True)
    for t, (b, c) in enumerate(upper_tiles(blocks)):
        for p in range(n_dp):
            hess[b * PANEL + p * part_rows : b * PANEL + (p + 1) * part_rows,
                 c * PANEL : (c + 1) * PANEL] = whole[0, p, t * part_rows : (t + 1) * part_rows, :]
    for c in range(blocks):
        low, high = c * PANEL, (c + 1) * PANEL
        out = jnp.dot(change[0, :, :high], hess[:high, low:high], preferred_element_type=F32)
        if high < columns:
            out = out + lax.dot_general(
                change[0, :, high:], hess[low:high, high:],
                (((1,), (1,)), ((), ())), preferred_element_type=F32,
            )
        hg_ref[0, :, low:high] = out * inverse


def per_device(tokens, expert_ids, weight_cols, uinv_panel, u_window, panel_index):
    n_expert, n_dp = lax.axis_size("expert"), lax.axis_size("dp")
    line = math.isqrt(n_expert // 2)
    dests = 2 * line
    rows, columns = weight_cols.shape[1:]
    n_tok, top_k = expert_ids.shape
    window = lax.dynamic_slice_in_dim(tokens, panel_index[0] * PANEL, columns, 1)
    blocks = columns // PANEL
    body = blocks * (blocks + 1) // 2 * (PANEL // n_dp)
    dma = pltpu.SemaphoreType.DMA
    vmem = pl.BlockSpec(memory_space=pltpu.VMEM)
    hbm = pl.BlockSpec(memory_space=pl.ANY)
    change, whole, cnt = pl.pallas_call(
        functools.partial(route_kernel, line, n_dp),
        out_shape=(
            jax.ShapeDtypeStruct((2, rows, columns), BF16),
            jax.ShapeDtypeStruct((2, n_dp, body, PANEL), BF16),
            jax.ShapeDtypeStruct((2, 8, PANEL), F32),
        ),
        in_specs=[vmem, vmem, hbm, hbm, hbm],
        out_specs=(vmem,) * 3,
        scratch_shapes=[
            pltpu.VMEM(weight_cols.shape, BF16),
            pltpu.VMEM(uinv_panel.shape, F32),
            pltpu.VMEM(u_window.shape, F32),
            pltpu.VMEM((line, n_tok, columns), BF16),
            pltpu.VMEM((line, top_k, n_tok), jnp.int32),
            pltpu.VMEM((2, dests, line // 2, 2 * SLOTS, columns), BF16),
            pltpu.VMEM((2, dests, line // 2, 2 * SLOTS, columns), BF16),
            pltpu.VMEM((2 * dests, 8, n_tok), F32),
            pltpu.VMEM((dests, 2, 8, n_tok), F32),
            pltpu.VMEM((2, n_dp, body + 16, PANEL), BF16),
            pltpu.VMEM((2, n_dp - 1, body + 16, PANEL), BF16),
            dma((3,)),
            dma((line,)), dma((line,)), dma, dma((line,)), dma((2,)), dma((2,)), dma, dma,
            dma((2, n_dp - 1)), dma((2, n_dp - 1)), dma((2, n_dp - 1)), dma((2, n_dp)),
        ],
        compiler_params=pltpu.CompilerParams(
            collective_id=0, has_side_effects=True, vmem_limit_bytes=32 * 1024 * 1024
        ),
    )(window, expert_ids.T, weight_cols, uinv_panel, u_window)

    def per_expert(*shape):
        return pl.BlockSpec((1,) + shape, lambda i: (i,) + (0,) * len(shape))

    return pl.pallas_call(
        functools.partial(last_kernel, n_dp),
        grid=(2,),
        out_shape=(
            jax.ShapeDtypeStruct((2, rows, PANEL), BF16),
            jax.ShapeDtypeStruct((2, rows, columns - PANEL), BF16),
            jax.ShapeDtypeStruct((2, rows, columns), F32),
        ),
        in_specs=[
            per_expert(rows, columns), per_expert(rows, columns),
            per_expert(n_dp, body, PANEL), per_expert(8, PANEL),
        ],
        out_specs=(per_expert(rows, PANEL), per_expert(rows, columns - PANEL), per_expert(rows, columns)),
        scratch_shapes=[pltpu.VMEM((columns, columns), BF16)],
        compiler_params=pltpu.CompilerParams(vmem_limit_bytes=16 * 1024 * 1024),
    )(weight_cols, change, whole, cnt)


def solution(mesh):
    placed = (
        P(("expert", "dp"), None),
        P(("expert", "dp"), None),
        P("expert", "dp", None),
        P("expert", None, None),
        P("expert", None, None),
        P(),
    )
    return jax.shard_map(
        per_device,
        mesh=mesh,
        in_specs=placed,
        out_specs=(P("expert", "dp", None), P("expert", "dp", None), P("expert", "dp", None)),
        check_vma=False,
    )
```

```python
import functools
import math

import jax
import jax.numpy as jnp
from jax import lax
from jax.experimental import pallas as pl
from jax.experimental.pallas import tpu as pltpu
from jax.sharding import PartitionSpec as P

PANEL = 128
SLOTS = 8
PIECES = 4
TWO_PI = 2.0 * math.pi
HIGHEST = lax.Precision.HIGHEST
MESH = pl.DeviceIdType.MESH
F32 = jnp.float32
BF16 = jnp.bfloat16


def sin_turn(turns):
    part = turns - jnp.round(turns)
    half = jnp.where(part < 0, -0.5, 0.5)
    part = jnp.where(jnp.abs(part) > 0.25, half - part, part)
    angle = part * TWO_PI
    square = angle * angle
    series = jnp.full_like(square, -1.0 / math.factorial(11))
    for power in (9, 7, 5, 3, 1):
        sign = 1.0 if power % 4 == 1 else -1.0
        series = series * square + sign / math.factorial(power)
    return angle * series


def tiles_of(blocks):
    last = blocks - 1
    return [(b, c) for b in range(last) for c in range(b, last)] + [(last, c) for c in range(blocks)]


def route_kernel(
    line, n_dp,
    win_ref, ids_ref, w_hbm, uinv_hbm, uw_hbm,
    change, whole, total_cnt,
    w_ref, uinv_ref, uw_ref, tok, idb, outb, inb, cnt_out, cnt_in, gram_out, gram_in,
    load_s, tok_s, tok_r, ids_s, ids_r, row_s, row_r, cnt_s, cnt_r, rs_s, rs_r, ag_s, ag_r,
):
    idx = lax.axis_index("expert")
    xpos = lax.axis_index("dp")
    core = idx % 2
    y = (idx // 2) % line
    z = idx // (2 * line)
    dests = 2 * line
    pairs = line // 2
    columns = w_ref.shape[2]
    blocks = columns // PANEL
    tiles = tiles_of(blocks)
    main = columns - PANEL
    part_rows = PANEL // n_dp
    body = len(tiles) * part_rows
    body_main = (len(tiles) - blocks) * part_rows
    tokens = tok.shape[1]
    own = line - 2

    loads = [
        pltpu.make_async_copy(w_hbm, w_ref, load_s.at[0]),
        pltpu.make_async_copy(uinv_hbm, uinv_ref, load_s.at[1]),
        pltpu.make_async_copy(uw_hbm, uw_ref, load_s.at[2]),
    ]
    for load in loads:
        load.start()

    stride1 = 2 * line - (2 * line - 2) * core
    place1 = z * (1 - core) + y * core
    base1 = idx - place1 * stride1
    stride2 = 2 + (2 * line - 2) * core
    place2 = y * (1 - core) + z * core
    base2 = idx - core - place2 * stride2
    self_dest = 2 * place2 + core
    my_slot = core * line + place2

    barrier = pltpu.get_barrier_semaphore()

    def greet(device, at=xpos):
        pl.semaphore_signal(barrier, inc=1, device_id=(device, at), device_id_type=MESH)

    @pl.loop(1, line)
    def _(d):
        greet(base1 + ((place1 + d) % line) * stride1)

    @pl.loop(1, line)
    def _(d):
        greet(base2 + ((place2 + d) % line) * stride2 + core)

    @pl.loop(0, line)
    def _(d):
        other = 1 - core
        stride = 2 + (2 * line - 2) * other
        place = y * (1 - other) + z * other
        greet(idx - core - place * stride + d * stride + other)

    @pl.loop(1, n_dp)
    def _(d):
        greet(idx, (xpos + d) % n_dp)

    tok[own] = win_ref[...]
    idb[own] = ids_ref[...]

    pl.semaphore_wait(barrier, 3 * line - 2 + n_dp - 1)

    right = (base1 + ((place1 + 1) % line) * stride1, xpos)
    left = (base1 + ((place1 + line - 1) % line) * stride1, xpos)

    for step in range(1, pairs + 1):
        for way in range(1 if step == pairs else 2):
            slot = 2 * (step - 1) + way + (1 if step == pairs else 0)
            at = (place1 + (step if way == 0 else line - step)) % line
            pltpu.make_async_remote_copy(
                ids_ref, idb.at[slot], ids_s, ids_r.at[slot],
                device_id=(base1 + at * stride1, xpos), device_id_type=MESH,
            ).start()

    piece_rows = tokens // PIECES

    def pieces_of(way, far):
        return range(way * PIECES // 2, (way + 1) * PIECES // 2) if far else range(PIECES)

    hops = []

    def start_hop(step, way, piece):
        source = own if step == 1 else 2 * (step - 2) + way
        target = line - 1 if step == pairs else 2 * (step - 1) + way
        rows = pl.ds(piece * piece_rows, piece_rows)
        copy = pltpu.make_async_remote_copy(
            tok.at[source, rows], tok.at[target, rows],
            tok_s.at[target, piece], tok_r.at[target, piece],
            device_id=right if way == 0 else left, device_id_type=MESH,
        )
        copy.start()
        hops.append(copy)

    for piece in range(PIECES):
        for way in range(2):
            if piece in pieces_of(way, pairs == 1):
                start_hop(1, way, piece)

    def weights(i):
        panel = w_ref[i, :, :PANEL].astype(F32)
        scale = (jnp.max(jnp.abs(panel), axis=1, keepdims=True) + 1e-6) / 7.0
        error = scale * sin_turn(panel / scale) * (1.0 / TWO_PI)
        change[i, :, :PANEL] = (-error).astype(BF16)
        left_part = jnp.dot(error, uinv_ref[i], precision=HIGHEST, preferred_element_type=F32)
        correction = jnp.dot(left_part, uw_ref[i], precision=HIGHEST, preferred_element_type=F32)
        change[i, :, PANEL:] = (-correction).astype(BF16)

    row = lax.broadcasted_iota(jnp.int32, (2 * dests, 2 * tokens), 0)
    named = (
        (row // 4) * (4 + (4 * line - 4) * core)
        + row % 4
        + (1 - core) * z * (4 * line)
        + core * y * 4
    )
    before = (
        lax.broadcasted_iota(jnp.int32, (2 * tokens, 2 * tokens), 0)
        < lax.broadcasted_iota(jnp.int32, (2 * tokens, 2 * tokens), 1)
    ).astype(F32).astype(BF16)
    slot_of = lax.broadcasted_iota(jnp.int32, (2 * SLOTS, 2 * tokens), 0).astype(F32)
    cnt_out[...] = jnp.zeros_like(cnt_out)

    def cut(group):
        return (pl.ds(0, columns), pl.ds(0, main), pl.ds(main, PANEL))[group]

    def send_rows(group, k, q):
        d = (self_dest + k) % dests
        i = 1 if group else 0
        pltpu.make_async_remote_copy(
            outb.at[i, d, q, :, cut(group)], inb.at[i, my_slot, q, :, cut(group)],
            row_s.at[group], row_r.at[group],
            device_id=(base2 + (d // 2) * stride2 + d % 2, xpos), device_id_type=MESH,
        ).start()

    def pick_rows(q):
        ids = jnp.concatenate([idb[2 * q], idb[2 * q + 1]], axis=1)
        member = jnp.zeros(named.shape, F32)
        for k in range(ids.shape[0]):
            member = member + jnp.where(ids[k : k + 1, :] == named, 1.0, 0.0)
        rank = jnp.dot(member.astype(BF16), before, preferred_element_type=F32)
        rank = jnp.where(member > 0.5, rank, -1.0)
        half = member[:, :tokens] + member[:, tokens:]
        cnt_out[...] += jnp.broadcast_to(half[:, None, :], cnt_out.shape)
        source = tok[pl.ds(2 * q, 2)].reshape(2 * tokens, columns)
        step = min(8, 2 * dests)
        for e in range(0, 2 * dests, step):
            pick = jnp.where(rank[e : e + step, None, :] == slot_of[None], 1.0, 0.0)
            pick = pick.reshape(step * 2 * SLOTS, 2 * tokens).astype(BF16)
            rows = jnp.dot(pick, source, preferred_element_type=F32).astype(BF16)
            rows = rows.reshape(step, 2 * SLOTS, -1)
            for m in range(step):
                outb[(e + m) % 2, (e + m) // 2, q] = rows[m]
        inb[0, my_slot, q] = outb[0, self_dest, q]
        inb[1, my_slot, q] = outb[1, self_dest, q]

        @pl.loop(1, dests)
        def _(k):
            send_rows(0, k, q)

    for q in range(pairs):
        last = q == pairs - 1
        for piece in range(PIECES):
            for way in range(2):
                if piece in pieces_of(way, last):
                    source = line - 1 if last else 2 * q + way
                    held = tok.at[source, pl.ds(piece * piece_rows, piece_rows)]
                    pltpu.make_async_copy(held, held, tok_r.at[source, piece]).wait()
                    if not last and piece in pieces_of(way, q + 2 == pairs):
                        start_hop(q + 2, way, piece)
        for source in range(2 * q, 2 * q + 2):
            if source != own:
                pltpu.make_async_copy(ids_ref, idb.at[source], ids_r.at[source]).wait()
        pick_rows(q)

    @pl.loop(1, dests)
    def _(k):
        d = (self_dest + k) % dests
        peer = (base2 + (d // 2) * stride2 + d % 2, xpos)
        pltpu.make_async_remote_copy(
            cnt_out.at[pl.ds(2 * d, 2)], cnt_in.at[my_slot], cnt_s, cnt_r,
            device_id=peer, device_id_type=MESH,
        ).start()

    for group in (1, 2):

        @pl.loop(1, dests)
        def _(k):
            send_rows(group, k, slice(None))

    cnt_in[my_slot] = cnt_out[pl.ds(2 * self_dest, 2)]

    def wait_rows(group, sem):
        view = inb.at[1 if group else 0, pl.ds(0, dests - 1), :, :, cut(group)]
        pltpu.make_async_copy(view, view, sem.at[group]).wait()

    def part(group, counts=True):
        first, size = ((0, body), (0, body_main), (body_main, body - body_main))[group]
        return pl.ds(first, size + (16 if counts and group == 2 else 0))

    def gram(group):
        wait_rows(group, row_r)
        i = 1 if group else 0
        wide = main if group == 1 else columns
        rows = inb[i, :, :, :, pl.ds(0, wide)].reshape(-1, wide)
        first = blocks - 1 if group == 2 else 0
        for b in range(first, blocks - 1 if group == 1 else blocks):
            start, stop = (0, columns) if b == blocks - 1 else (b * PANEL, main)
            product = lax.dot_general(
                rows[:, b * PANEL : (b + 1) * PANEL], rows[:, start:stop],
                (((0,), (0,)), ((), ())), preferred_element_type=F32,
            ).astype(BF16)
            for c in range(start // PANEL, stop // PANEL):
                t = tiles.index((b, c))
                for p in range(n_dp):
                    gram_out[i, p, t * part_rows : (t + 1) * part_rows, :] = product[
                        p * part_rows : (p + 1) * part_rows,
                        c * PANEL - start : (c + 1) * PANEL - start,
                    ]
        if group == 2:
            view = cnt_in.at[pl.ds(0, dests - 1)]
            pltpu.make_async_copy(view, view, cnt_r).wait()
            count = jnp.sum(cnt_in[...], axis=0).reshape(16, PANEL).astype(BF16)
            for p in range(n_dp):
                gram_out[i, p, body:, :] = count
        for d in range(1, n_dp):
            other = (xpos + d) % n_dp
            pltpu.make_async_remote_copy(
                gram_out.at[i, other, part(group)], gram_in.at[i, d - 1, part(group)],
                rs_s.at[group, d - 1], rs_r.at[group, d - 1],
                device_id=(idx, other), device_id_type=MESH,
            ).start()

    def wait_shares(group, sem):
        for d in range(1, n_dp):
            view = gram_in.at[1 if group else 0, d - 1, part(group)]
            pltpu.make_async_copy(view, view, sem.at[group, d - 1]).wait()

    def share(group):
        wait_shares(group, rs_r)
        i = 1 if group else 0
        total = gram_out[i, xpos, part(group)].astype(F32)
        for d in range(1, n_dp):
            total = total + gram_in[i, d - 1, part(group)].astype(F32)
        mine = part(group, False)
        whole[i, xpos, mine] = total[: mine.size].astype(BF16)
        for d in range(1, n_dp):
            other = (xpos + d) % n_dp
            pltpu.make_async_remote_copy(
                whole.at[i, xpos, mine], whole.at[i, xpos, mine],
                ag_s.at[group, d - 1], ag_r.at[group, d - 1],
                device_id=(idx, other), device_id_type=MESH,
            ).start()
        if group == 2:
            total_cnt[...] = total[mine.size :].reshape(2, 8, PANEL)

    def wait_whole(group, sem):
        for d in range(1, n_dp):
            view = whole.at[1 if group else 0, (xpos + n_dp - d) % n_dp, part(group, False)]
            pltpu.make_async_copy(view, view, sem.at[group, d - 1]).wait()

    for load in loads:
        load.wait()
    weights(0)
    weights(1)
    gram(0)
    share(0)
    gram(1)
    gram(2)
    share(1)
    share(2)
    for group in range(3):
        wait_whole(group, ag_r)

    for group in range(3):
        wait_rows(group, row_s)
        wait_shares(group, rs_s)
        wait_whole(group, ag_s)
    view = cnt_in.at[pl.ds(0, dests - 1)]
    pltpu.make_async_copy(view, view, cnt_s).wait()
    for copy in hops:
        copy.wait_send()
    view = idb.at[pl.ds(0, line - 1)]
    pltpu.make_async_copy(view, view, ids_s).wait()


def last_kernel(n_dp, w_ref, change, whole, cnt, q_ref, ww_ref, hg_ref, hess):
    columns = w_ref.shape[2]
    blocks = columns // PANEL
    part_rows = PANEL // n_dp
    weights = w_ref[0].astype(F32) + change[0].astype(F32)
    q_ref[0] = weights[:, :PANEL].astype(BF16)
    ww_ref[0] = weights[:, PANEL:].astype(BF16)
    inverse = 1.0 / jnp.sum(cnt[0, :1], axis=1, keepdims=True)
    main = columns - PANEL
    for t, (b, c) in enumerate(tiles_of(blocks)):
        for p in range(n_dp):
            hess[b * PANEL + p * part_rows : b * PANEL + (p + 1) * part_rows,
                 c * PANEL : (c + 1) * PANEL] = whole[0, p, t * part_rows : (t + 1) * part_rows, :]
    def across(left, right):
        return lax.dot_general(left, right, (((1,), (1,)), ((), ())), preferred_element_type=F32)

    for c in range(blocks - 1):
        low, high = c * PANEL, (c + 1) * PANEL
        out = jnp.dot(change[0, :, :high], hess[:high, low:high], preferred_element_type=F32)
        out = out + jnp.dot(change[0, :, main:], hess[main:, low:high], preferred_element_type=F32)
        if high < main:
            out = out + across(change[0, :, high:main], hess[low:high, high:main])
        hg_ref[0, :, low:high] = out * inverse
    hg_ref[0, :, main:] = across(change[0], hess[main:]) * inverse


def per_device(tokens, expert_ids, weight_cols, uinv_panel, u_window, panel_index):
    n_expert, n_dp = lax.axis_size("expert"), lax.axis_size("dp")
    line = math.isqrt(n_expert // 2)
    dests = 2 * line
    rows, columns = weight_cols.shape[1:]
    n_tok, top_k = expert_ids.shape
    window = lax.dynamic_slice_in_dim(tokens, panel_index[0] * PANEL, columns, 1)
    blocks = columns // PANEL
    body = blocks * (blocks + 1) // 2 * (PANEL // n_dp)
    dma = pltpu.SemaphoreType.DMA
    vmem = pl.BlockSpec(memory_space=pltpu.VMEM)
    hbm = pl.BlockSpec(memory_space=pl.ANY)
    change, whole, cnt = pl.pallas_call(
        functools.partial(route_kernel, line, n_dp),
        out_shape=(
            jax.ShapeDtypeStruct((2, rows, columns), BF16),
            jax.ShapeDtypeStruct((2, n_dp, body, PANEL), BF16),
            jax.ShapeDtypeStruct((2, 8, PANEL), F32),
        ),
        in_specs=[vmem, vmem, hbm, hbm, hbm],
        out_specs=(vmem,) * 3,
        scratch_shapes=[
            pltpu.VMEM(weight_cols.shape, BF16),
            pltpu.VMEM(uinv_panel.shape, F32),
            pltpu.VMEM(u_window.shape, F32),
            pltpu.VMEM((line, n_tok, columns), BF16),
            pltpu.VMEM((line, top_k, n_tok), jnp.int32),
            pltpu.VMEM((2, dests, line // 2, 2 * SLOTS, columns), BF16),
            pltpu.VMEM((2, dests, line // 2, 2 * SLOTS, columns), BF16),
            pltpu.VMEM((2 * dests, 8, n_tok), F32),
            pltpu.VMEM((dests, 2, 8, n_tok), F32),
            pltpu.VMEM((2, n_dp, body + 16, PANEL), BF16),
            pltpu.VMEM((2, n_dp - 1, body + 16, PANEL), BF16),
            dma((3,)),
            dma((line, PIECES)), dma((line, PIECES)), dma, dma((line,)), dma((3,)), dma((3,)), dma, dma,
            dma((3, n_dp - 1)), dma((3, n_dp - 1)), dma((3, n_dp - 1)), dma((3, n_dp - 1)),
        ],
        compiler_params=pltpu.CompilerParams(
            collective_id=0, has_side_effects=True, vmem_limit_bytes=56 * 1024 * 1024
        ),
    )(window, expert_ids.T, weight_cols, uinv_panel, u_window)

    def per_expert(*shape):
        return pl.BlockSpec((1,) + shape, lambda i: (i,) + (0,) * len(shape))

    return pl.pallas_call(
        functools.partial(last_kernel, n_dp),
        grid=(2,),
        out_shape=(
            jax.ShapeDtypeStruct((2, rows, PANEL), BF16),
            jax.ShapeDtypeStruct((2, rows, columns - PANEL), BF16),
            jax.ShapeDtypeStruct((2, rows, columns), F32),
        ),
        in_specs=[
            per_expert(rows, columns), per_expert(rows, columns),
            per_expert(n_dp, body, PANEL), per_expert(8, PANEL),
        ],
        out_specs=(per_expert(rows, PANEL), per_expert(rows, columns - PANEL), per_expert(rows, columns)),
        scratch_shapes=[pltpu.VMEM((columns, columns), BF16)],
        compiler_params=pltpu.CompilerParams(vmem_limit_bytes=16 * 1024 * 1024),
    )(weight_cols, change, whole, cnt)


def solution(mesh):
    placed = (
        P(("expert", "dp"), None),
        P(("expert", "dp"), None),
        P("expert", "dp", None),
        P("expert", None, None),
        P("expert", None, None),
        P(),
    )
    return jax.shard_map(
        per_device,
        mesh=mesh,
        in_specs=placed,
        out_specs=(P("expert", "dp", None), P("expert", "dp", None), P("expert", "dp", None)),
        check_vma=False,
    )
```

```python
import functools
import math

import jax
import jax.numpy as jnp
from jax import lax
from jax.experimental import pallas as pl
from jax.experimental.pallas import tpu as pltpu
from jax.sharding import PartitionSpec as P

PANEL = 128
SLOTS = 8
PIECES = 4
TWO_PI = 2.0 * math.pi
HIGHEST = lax.Precision.HIGHEST
MESH = pl.DeviceIdType.MESH
F32 = jnp.float32
BF16 = jnp.bfloat16


def sin_turn(turns):
    part = turns - jnp.round(turns)
    half = jnp.where(part < 0, -0.5, 0.5)
    part = jnp.where(jnp.abs(part) > 0.25, half - part, part)
    angle = part * TWO_PI
    square = angle * angle
    series = jnp.full_like(square, -1.0 / math.factorial(11))
    for power in (9, 7, 5, 3, 1):
        sign = 1.0 if power % 4 == 1 else -1.0
        series = series * square + sign / math.factorial(power)
    return angle * series


def tiles_of(blocks):
    last = blocks - 1
    return [(b, c) for b in range(last) for c in range(b, last)] + [(last, c) for c in range(blocks)]


def route_kernel(
    line, n_dp,
    win_ref, ids_ref, w_hbm, uinv_hbm, uw_hbm,
    change, whole, total_cnt,
    w_ref, uinv_ref, uw_ref, tok, idb, outb, inb, cnt_out, cnt_in, gram_out, gram_in,
    load_s, tok_s, tok_r, ids_s, ids_r, row_s, row_r, cnt_s, cnt_r, rs_s, rs_r, ag_s, ag_r,
):
    idx = lax.axis_index("expert")
    xpos = lax.axis_index("dp")
    core = idx % 2
    y = (idx // 2) % line
    z = idx // (2 * line)
    dests = 2 * line
    pairs = line // 2
    columns = w_ref.shape[2]
    blocks = columns // PANEL
    tiles = tiles_of(blocks)
    main = columns - PANEL
    part_rows = PANEL // n_dp
    body = len(tiles) * part_rows
    body_main = (len(tiles) - blocks) * part_rows
    tokens = tok.shape[1]
    own = line - 2

    loads = [
        pltpu.make_async_copy(w_hbm, w_ref, load_s.at[0]),
        pltpu.make_async_copy(uinv_hbm, uinv_ref, load_s.at[1]),
        pltpu.make_async_copy(uw_hbm, uw_ref, load_s.at[2]),
    ]
    for load in loads:
        load.start()

    stride1 = 2 * line - (2 * line - 2) * core
    place1 = z * (1 - core) + y * core
    base1 = idx - place1 * stride1
    stride2 = 2 + (2 * line - 2) * core
    place2 = y * (1 - core) + z * core
    base2 = idx - core - place2 * stride2
    self_dest = 2 * place2 + core
    my_slot = core * line + place2

    barrier = pltpu.get_barrier_semaphore()

    def greet(device, at=xpos):
        pl.semaphore_signal(barrier, inc=1, device_id=(device, at), device_id_type=MESH)

    @pl.loop(1, line)
    def _(d):
        greet(base1 + ((place1 + d) % line) * stride1)

    @pl.loop(1, line)
    def _(d):
        greet(base2 + ((place2 + d) % line) * stride2 + core)

    @pl.loop(0, line)
    def _(d):
        other = 1 - core
        stride = 2 + (2 * line - 2) * other
        place = y * (1 - other) + z * other
        greet(idx - core - place * stride + d * stride + other)

    @pl.loop(1, n_dp)
    def _(d):
        greet(idx, (xpos + d) % n_dp)

    tok[own] = win_ref[...]
    idb[own] = ids_ref[...]

    pl.semaphore_wait(barrier, 3 * line - 2 + n_dp - 1)

    right = (base1 + ((place1 + 1) % line) * stride1, xpos)
    left = (base1 + ((place1 + line - 1) % line) * stride1, xpos)

    for step in range(1, pairs + 1):
        for way in range(1 if step == pairs else 2):
            slot = 2 * (step - 1) + way + (1 if step == pairs else 0)
            at = (place1 + (step if way == 0 else line - step)) % line
            pltpu.make_async_remote_copy(
                ids_ref, idb.at[slot], ids_s, ids_r.at[slot],
                device_id=(base1 + at * stride1, xpos), device_id_type=MESH,
            ).start()

    piece_rows = tokens // PIECES

    def pieces_of(way, far):
        return range(way * PIECES // 2, (way + 1) * PIECES // 2) if far else range(PIECES)

    hops = []

    def start_hop(step, way, piece):
        source = own if step == 1 else 2 * (step - 2) + way
        target = line - 1 if step == pairs else 2 * (step - 1) + way
        rows = pl.ds(piece * piece_rows, piece_rows)
        copy = pltpu.make_async_remote_copy(
            tok.at[source, rows], tok.at[target, rows],
            tok_s.at[target, piece], tok_r.at[target, piece],
            device_id=right if way == 0 else left, device_id_type=MESH,
        )
        copy.start()
        hops.append(copy)

    for piece in range(PIECES):
        for way in range(2):
            if piece in pieces_of(way, pairs == 1):
                start_hop(1, way, piece)

    def weights(i):
        panel = w_ref[i, :, :PANEL].astype(F32)
        scale = (jnp.max(jnp.abs(panel), axis=1, keepdims=True) + 1e-6) / 7.0
        error = scale * sin_turn(panel / scale) * (1.0 / TWO_PI)
        change[i, :, :PANEL] = (-error).astype(BF16)
        left_part = jnp.dot(error, uinv_ref[i], precision=HIGHEST, preferred_element_type=F32)
        correction = jnp.dot(left_part, uw_ref[i], precision=HIGHEST, preferred_element_type=F32)
        change[i, :, PANEL:] = (-correction).astype(BF16)

    row = lax.broadcasted_iota(jnp.int32, (2 * dests, 2 * tokens), 0)
    named = (
        (row // 4) * (4 + (4 * line - 4) * core)
        + row % 4
        + (1 - core) * z * (4 * line)
        + core * y * 4
    )
    before = (
        lax.broadcasted_iota(jnp.int32, (2 * tokens, 2 * tokens), 0)
        < lax.broadcasted_iota(jnp.int32, (2 * tokens, 2 * tokens), 1)
    ).astype(F32).astype(BF16)
    slot_of = lax.broadcasted_iota(jnp.int32, (2 * SLOTS, 2 * tokens), 0).astype(F32)
    cnt_out[...] = jnp.zeros_like(cnt_out)

    def cut(group):
        return (pl.ds(0, columns), pl.ds(0, main), pl.ds(main, PANEL))[group]

    def send_rows(group, k, q):
        d = (self_dest + k) % dests
        i = 1 if group else 0
        pltpu.make_async_remote_copy(
            outb.at[i, d, q, :, cut(group)], inb.at[i, my_slot, q, :, cut(group)],
            row_s.at[group], row_r.at[group],
            device_id=(base2 + (d // 2) * stride2 + d % 2, xpos), device_id_type=MESH,
        ).start()

    def pick_rows(q):
        ids = jnp.concatenate([idb[2 * q], idb[2 * q + 1]], axis=1)
        member = jnp.zeros(named.shape, F32)
        for k in range(ids.shape[0]):
            member = member + jnp.where(ids[k : k + 1, :] == named, 1.0, 0.0)
        rank = jnp.dot(member.astype(BF16), before, preferred_element_type=F32)
        rank = jnp.where(member > 0.5, rank, -1.0)
        half = member[:, :tokens] + member[:, tokens:]
        cnt_out[...] += jnp.broadcast_to(half[:, None, :], cnt_out.shape)
        source = tok[pl.ds(2 * q, 2)].reshape(2 * tokens, columns)
        step = min(8, 2 * dests)
        for e in range(0, 2 * dests, step):
            pick = jnp.where(rank[e : e + step, None, :] == slot_of[None], 1.0, 0.0)
            pick = pick.reshape(step * 2 * SLOTS, 2 * tokens).astype(BF16)
            rows = jnp.dot(pick, source, preferred_element_type=F32).astype(BF16)
            rows = rows.reshape(step, 2 * SLOTS, -1)
            for m in range(step):
                outb[(e + m) % 2, (e + m) // 2, q] = rows[m]
        inb[0, my_slot, q] = outb[0, self_dest, q]
        inb[1, my_slot, q] = outb[1, self_dest, q]

        for r in ([q - 1] if q < pairs - 1 else [q - 1, q]) if q else []:

            @pl.loop(1, dests)
            def _(k):
                send_rows(0, k, r)

    for q in range(pairs):
        last = q == pairs - 1
        for piece in range(PIECES):
            for way in range(2):
                if piece in pieces_of(way, last):
                    source = line - 1 if last else 2 * q + way
                    held = tok.at[source, pl.ds(piece * piece_rows, piece_rows)]
                    pltpu.make_async_copy(held, held, tok_r.at[source, piece]).wait()
                    if not last and piece in pieces_of(way, q + 2 == pairs):
                        start_hop(q + 2, way, piece)
        for source in range(2 * q, 2 * q + 2):
            if source != own:
                pltpu.make_async_copy(ids_ref, idb.at[source], ids_r.at[source]).wait()
        pick_rows(q)

    @pl.loop(1, dests)
    def _(k):
        d = (self_dest + k) % dests
        peer = (base2 + (d // 2) * stride2 + d % 2, xpos)
        pltpu.make_async_remote_copy(
            cnt_out.at[pl.ds(2 * d, 2)], cnt_in.at[my_slot], cnt_s, cnt_r,
            device_id=peer, device_id_type=MESH,
        ).start()

    @pl.loop(1, dests)
    def _(k):
        send_rows(1, k, pl.ds(0, pairs))

    cnt_in[my_slot] = cnt_out[pl.ds(2 * self_dest, 2)]

    def wait_rows(group, sem):
        view = inb.at[1 if group else 0, pl.ds(0, dests - 1), :, :, cut(group)]
        pltpu.make_async_copy(view, view, sem.at[group]).wait()

    def part(group, counts=True):
        first, size = ((0, body), (0, body_main), (body_main, body - body_main))[group]
        return pl.ds(first, size + (16 if counts and group == 2 else 0))

    def gram(group):
        wait_rows(group, row_r)
        i = 1 if group else 0
        wide = main if group == 1 else columns
        rows = inb[i, :, :, :, pl.ds(0, wide)].reshape(-1, wide)
        first = blocks - 1 if group == 2 else 0
        for b in range(first, blocks - 1 if group == 1 else blocks):
            start, stop = (0, columns) if b == blocks - 1 else (b * PANEL, main)
            product = lax.dot_general(
                rows[:, b * PANEL : (b + 1) * PANEL], rows[:, start:stop],
                (((0,), (0,)), ((), ())), preferred_element_type=F32,
            ).astype(BF16)
            for c in range(start // PANEL, stop // PANEL):
                t = tiles.index((b, c))
                for p in range(n_dp):
                    gram_out[i, p, t * part_rows : (t + 1) * part_rows, :] = product[
                        p * part_rows : (p + 1) * part_rows,
                        c * PANEL - start : (c + 1) * PANEL - start,
                    ]
        if group == 2:
            view = cnt_in.at[pl.ds(0, dests - 1)]
            pltpu.make_async_copy(view, view, cnt_r).wait()
            count = jnp.sum(cnt_in[...], axis=0).reshape(16, PANEL).astype(BF16)
            for p in range(n_dp):
                gram_out[i, p, body:, :] = count
        for d in range(1, n_dp):
            other = (xpos + d) % n_dp
            pltpu.make_async_remote_copy(
                gram_out.at[i, other, part(group)], gram_in.at[i, d - 1, part(group)],
                rs_s.at[group, d - 1], rs_r.at[group, d - 1],
                device_id=(idx, other), device_id_type=MESH,
            ).start()

    def wait_shares(group, sem):
        for d in range(1, n_dp):
            view = gram_in.at[1 if group else 0, d - 1, part(group)]
            pltpu.make_async_copy(view, view, sem.at[group, d - 1]).wait()

    def share(group):
        wait_shares(group, rs_r)
        i = 1 if group else 0
        total = gram_out[i, xpos, part(group)].astype(F32)
        for d in range(1, n_dp):
            total = total + gram_in[i, d - 1, part(group)].astype(F32)
        mine = part(group, False)
        whole[i, xpos, mine] = total[: mine.size].astype(BF16)
        for d in range(1, n_dp):
            other = (xpos + d) % n_dp
            pltpu.make_async_remote_copy(
                whole.at[i, xpos, mine], whole.at[i, xpos, mine],
                ag_s.at[group, d - 1], ag_r.at[group, d - 1],
                device_id=(idx, other), device_id_type=MESH,
            ).start()
        if group == 2:
            total_cnt[...] = total[mine.size :].reshape(2, 8, PANEL)

    def wait_whole(group, sem):
        for d in range(1, n_dp):
            view = whole.at[1 if group else 0, (xpos + n_dp - d) % n_dp, part(group, False)]
            pltpu.make_async_copy(view, view, sem.at[group, d - 1]).wait()

    for load in loads:
        load.wait()
    weights(0)
    weights(1)
    gram(0)
    share(0)

    @pl.loop(1, dests)
    def _(k):
        send_rows(2, k, pl.ds(0, pairs))

    gram(1)
    gram(2)
    share(1)
    share(2)
    for group in range(3):
        wait_whole(group, ag_r)

    for group in range(3):
        wait_rows(group, row_s)
        wait_shares(group, rs_s)
        wait_whole(group, ag_s)
    view = cnt_in.at[pl.ds(0, dests - 1)]
    pltpu.make_async_copy(view, view, cnt_s).wait()
    for copy in hops:
        copy.wait_send()
    view = idb.at[pl.ds(0, line - 1)]
    pltpu.make_async_copy(view, view, ids_s).wait()


def last_kernel(n_dp, w_ref, change, whole, cnt, q_ref, ww_ref, hg_ref, hess):
    columns = w_ref.shape[2]
    blocks = columns // PANEL
    part_rows = PANEL // n_dp
    weights = w_ref[0].astype(F32) + change[0].astype(F32)
    q_ref[0] = weights[:, :PANEL].astype(BF16)
    ww_ref[0] = weights[:, PANEL:].astype(BF16)
    inverse = 1.0 / jnp.sum(cnt[0, :1], axis=1, keepdims=True)
    main = columns - PANEL
    for t, (b, c) in enumerate(tiles_of(blocks)):
        for p in range(n_dp):
            hess[b * PANEL + p * part_rows : b * PANEL + (p + 1) * part_rows,
                 c * PANEL : (c + 1) * PANEL] = whole[0, p, t * part_rows : (t + 1) * part_rows, :]
    def across(left, right):
        return lax.dot_general(left, right, (((1,), (1,)), ((), ())), preferred_element_type=F32)

    for c in range(blocks - 1):
        low, high = c * PANEL, (c + 1) * PANEL
        out = jnp.dot(change[0, :, :high], hess[:high, low:high], preferred_element_type=F32)
        out = out + jnp.dot(change[0, :, main:], hess[main:, low:high], preferred_element_type=F32)
        if high < main:
            out = out + across(change[0, :, high:main], hess[low:high, high:main])
        hg_ref[0, :, low:high] = out * inverse
    hg_ref[0, :, main:] = across(change[0], hess[main:]) * inverse


def per_device(tokens, expert_ids, weight_cols, uinv_panel, u_window, panel_index):
    n_expert, n_dp = lax.axis_size("expert"), lax.axis_size("dp")
    line = math.isqrt(n_expert // 2)
    dests = 2 * line
    rows, columns = weight_cols.shape[1:]
    n_tok, top_k = expert_ids.shape
    window = lax.dynamic_slice_in_dim(tokens, panel_index[0] * PANEL, columns, 1)
    blocks = columns // PANEL
    body = blocks * (blocks + 1) // 2 * (PANEL // n_dp)
    dma = pltpu.SemaphoreType.DMA
    vmem = pl.BlockSpec(memory_space=pltpu.VMEM)
    hbm = pl.BlockSpec(memory_space=pl.ANY)
    change, whole, cnt = pl.pallas_call(
        functools.partial(route_kernel, line, n_dp),
        out_shape=(
            jax.ShapeDtypeStruct((2, rows, columns), BF16),
            jax.ShapeDtypeStruct((2, n_dp, body, PANEL), BF16),
            jax.ShapeDtypeStruct((2, 8, PANEL), F32),
        ),
        in_specs=[vmem, vmem, hbm, hbm, hbm],
        out_specs=(vmem,) * 3,
        scratch_shapes=[
            pltpu.VMEM(weight_cols.shape, BF16),
            pltpu.VMEM(uinv_panel.shape, F32),
            pltpu.VMEM(u_window.shape, F32),
            pltpu.VMEM((line, n_tok, columns), BF16),
            pltpu.VMEM((line, top_k, n_tok), jnp.int32),
            pltpu.VMEM((2, dests, line // 2, 2 * SLOTS, columns), BF16),
            pltpu.VMEM((2, dests, line // 2, 2 * SLOTS, columns), BF16),
            pltpu.VMEM((2 * dests, 8, n_tok), F32),
            pltpu.VMEM((dests, 2, 8, n_tok), F32),
            pltpu.VMEM((2, n_dp, body + 16, PANEL), BF16),
            pltpu.VMEM((2, n_dp - 1, body + 16, PANEL), BF16),
            dma((3,)),
            dma((line, PIECES)), dma((line, PIECES)), dma, dma((line,)), dma((3,)), dma((3,)), dma, dma,
            dma((3, n_dp - 1)), dma((3, n_dp - 1)), dma((3, n_dp - 1)), dma((3, n_dp - 1)),
        ],
        compiler_params=pltpu.CompilerParams(
            collective_id=0, has_side_effects=True, vmem_limit_bytes=56 * 1024 * 1024
        ),
    )(window, expert_ids.T, weight_cols, uinv_panel, u_window)

    def per_expert(*shape):
        return pl.BlockSpec((1,) + shape, lambda i: (i,) + (0,) * len(shape))

    return pl.pallas_call(
        functools.partial(last_kernel, n_dp),
        grid=(2,),
        out_shape=(
            jax.ShapeDtypeStruct((2, rows, PANEL), BF16),
            jax.ShapeDtypeStruct((2, rows, columns - PANEL), BF16),
            jax.ShapeDtypeStruct((2, rows, columns), F32),
        ),
        in_specs=[
            per_expert(rows, columns), per_expert(rows, columns),
            per_expert(n_dp, body, PANEL), per_expert(8, PANEL),
        ],
        out_specs=(per_expert(rows, PANEL), per_expert(rows, columns - PANEL), per_expert(rows, columns)),
        scratch_shapes=[pltpu.VMEM((columns, columns), BF16)],
        compiler_params=pltpu.CompilerParams(vmem_limit_bytes=56 * 1024 * 1024),
    )(weight_cols, change, whole, cnt)


def solution(mesh):
    placed = (
        P(("expert", "dp"), None),
        P(("expert", "dp"), None),
        P("expert", "dp", None),
        P("expert", None, None),
        P("expert", None, None),
        P(),
    )
    return jax.shard_map(
        per_device,
        mesh=mesh,
        in_specs=placed,
        out_specs=(P("expert", "dp", None), P("expert", "dp", None), P("expert", "dp", None)),
        check_vma=False,
    )
```

```python
import functools
import math

import jax
import jax.numpy as jnp
from jax import lax
from jax.experimental import pallas as pl
from jax.experimental.pallas import tpu as pltpu
from jax.sharding import PartitionSpec as P

PANEL = 128
SLOTS = 8
PIECES = 4
TWO_PI = 2.0 * math.pi
HIGHEST = lax.Precision.HIGHEST
MESH = pl.DeviceIdType.MESH
F32 = jnp.float32
BF16 = jnp.bfloat16


def sin_turn(turns):
    part = turns - jnp.round(turns)
    half = jnp.where(part < 0, -0.5, 0.5)
    part = jnp.where(jnp.abs(part) > 0.25, half - part, part)
    angle = part * TWO_PI
    square = angle * angle
    series = jnp.full_like(square, -1.0 / math.factorial(11))
    for power in (9, 7, 5, 3, 1):
        sign = 1.0 if power % 4 == 1 else -1.0
        series = series * square + sign / math.factorial(power)
    return angle * series


def tiles_of(blocks):
    last = blocks - 1
    return [(b, c) for b in range(last) for c in range(b, last)] + [(last, c) for c in range(blocks)]


def route_kernel(
    line, n_dp,
    win_ref, ids_ref, w_hbm, uinv_hbm, uw_hbm,
    change, whole, total_cnt,
    w_ref, uinv_ref, uw_ref, tok, idb, outb, inb, cnt_out, cnt_in, gram_out, gram_in,
    load_s, tok_s, tok_r, ids_s, ids_r, row_s, row_r, cnt_s, cnt_r, rs_s, rs_r, ag_s, ag_r,
):
    idx = lax.axis_index("expert")
    xpos = lax.axis_index("dp")
    core = idx % 2
    y = (idx // 2) % line
    z = idx // (2 * line)
    dests = 2 * line
    pairs = line // 2
    columns = w_ref.shape[2]
    blocks = columns // PANEL
    tiles = tiles_of(blocks)
    main = columns - PANEL
    part_rows = PANEL // n_dp
    body = len(tiles) * part_rows
    body_main = (len(tiles) - blocks) * part_rows
    tokens = tok.shape[1]
    own = line - 2

    loads = [
        pltpu.make_async_copy(w_hbm, w_ref, load_s.at[0]),
        pltpu.make_async_copy(uinv_hbm, uinv_ref, load_s.at[1]),
        pltpu.make_async_copy(uw_hbm, uw_ref, load_s.at[2]),
    ]
    for load in loads:
        load.start()

    stride1 = 2 * line - (2 * line - 2) * core
    place1 = z * (1 - core) + y * core
    base1 = idx - place1 * stride1
    stride2 = 2 + (2 * line - 2) * core
    place2 = y * (1 - core) + z * core
    base2 = idx - core - place2 * stride2
    self_dest = 2 * place2 + core
    my_slot = core * line + place2

    barrier = pltpu.get_barrier_semaphore()

    def greet(device, at=xpos):
        pl.semaphore_signal(barrier, inc=1, device_id=(device, at), device_id_type=MESH)

    @pl.loop(1, line)
    def _(d):
        greet(base1 + ((place1 + d) % line) * stride1)

    @pl.loop(1, line)
    def _(d):
        greet(base2 + ((place2 + d) % line) * stride2 + core)

    @pl.loop(0, line)
    def _(d):
        other = 1 - core
        stride = 2 + (2 * line - 2) * other
        place = y * (1 - other) + z * other
        greet(idx - core - place * stride + d * stride + other)

    @pl.loop(1, n_dp)
    def _(d):
        greet(idx, (xpos + d) % n_dp)

    tok[own] = win_ref[...]
    idb[own] = ids_ref[...]

    pl.semaphore_wait(barrier, 3 * line - 2 + n_dp - 1)

    right = (base1 + ((place1 + 1) % line) * stride1, xpos)
    left = (base1 + ((place1 + line - 1) % line) * stride1, xpos)

    piece_rows = tokens // PIECES

    def pieces_of(way, far):
        return range(way * PIECES // 2, (way + 1) * PIECES // 2) if far else range(PIECES)

    hops = []

    def start_hop(step, way, piece):
        source = own if step == 1 else 2 * (step - 2) + way
        target = line - 1 if step == pairs else 2 * (step - 1) + way
        rows = pl.ds(piece * piece_rows, piece_rows)
        copy = pltpu.make_async_remote_copy(
            tok.at[source, rows], tok.at[target, rows],
            tok_s.at[target, piece], tok_r.at[target, piece],
            device_id=right if way == 0 else left, device_id_type=MESH,
        )
        copy.start()
        hops.append(copy)

    for piece in range(PIECES):
        for way in range(2):
            if piece in pieces_of(way, pairs == 1):
                start_hop(1, way, piece)

    for step in range(1, pairs + 1):
        for way in range(1 if step == pairs else 2):
            slot = 2 * (step - 1) + way + (1 if step == pairs else 0)
            at = (place1 + (step if way == 0 else line - step)) % line
            pltpu.make_async_remote_copy(
                ids_ref, idb.at[slot], ids_s, ids_r.at[slot],
                device_id=(base1 + at * stride1, xpos), device_id_type=MESH,
            ).start()

    def weights(i):
        panel = w_ref[i, :, :PANEL].astype(F32)
        scale = (jnp.max(jnp.abs(panel), axis=1, keepdims=True) + 1e-6) / 7.0
        error = scale * sin_turn(panel / scale) * (1.0 / TWO_PI)
        change[i, :, :PANEL] = (-error).astype(BF16)
        left_part = jnp.dot(error, uinv_ref[i], precision=HIGHEST, preferred_element_type=F32)
        correction = jnp.dot(left_part, uw_ref[i], precision=HIGHEST, preferred_element_type=F32)
        change[i, :, PANEL:] = (-correction).astype(BF16)

    row = lax.broadcasted_iota(jnp.int32, (2 * dests, 2 * tokens), 0)
    named = (
        (row // 4) * (4 + (4 * line - 4) * core)
        + row % 4
        + (1 - core) * z * (4 * line)
        + core * y * 4
    )
    before = (
        lax.broadcasted_iota(jnp.int32, (2 * tokens, 2 * tokens), 0)
        < lax.broadcasted_iota(jnp.int32, (2 * tokens, 2 * tokens), 1)
    ).astype(F32).astype(BF16)
    slot_of = lax.broadcasted_iota(jnp.int32, (2 * SLOTS, 2 * tokens), 0).astype(F32)
    cnt_out[...] = jnp.zeros_like(cnt_out)

    def cut(group):
        return (pl.ds(0, columns), pl.ds(0, main), pl.ds(main, PANEL))[group]

    def send_rows(group, k, q):
        d = (self_dest + k) % dests
        i = 1 if group else 0
        pltpu.make_async_remote_copy(
            outb.at[i, d, q, :, cut(group)], inb.at[i, my_slot, q, :, cut(group)],
            row_s.at[group], row_r.at[group],
            device_id=(base2 + (d // 2) * stride2 + d % 2, xpos), device_id_type=MESH,
        ).start()

    def pick_rows(q):
        ids = jnp.concatenate([idb[2 * q], idb[2 * q + 1]], axis=1)
        member = jnp.zeros(named.shape, F32)
        for k in range(ids.shape[0]):
            member = member + jnp.where(ids[k : k + 1, :] == named, 1.0, 0.0)
        rank = jnp.dot(member.astype(BF16), before, preferred_element_type=F32)
        rank = jnp.where(member > 0.5, rank, -1.0)
        half = member[:, :tokens] + member[:, tokens:]
        for d in range(dests):
            cnt_out[d, 0:2] += half[2 * d : 2 * d + 2]
        source = tok[pl.ds(2 * q, 2)].reshape(2 * tokens, columns)
        step = min(8, 2 * dests)
        for e in range(0, 2 * dests, step):
            pick = jnp.where(rank[e : e + step, None, :] == slot_of[None], 1.0, 0.0)
            pick = pick.reshape(step * 2 * SLOTS, 2 * tokens).astype(BF16)
            rows = jnp.dot(pick, source, preferred_element_type=F32).astype(BF16)
            rows = rows.reshape(step, 2 * SLOTS, -1)
            for m in range(step):
                outb[(e + m) % 2, (e + m) // 2, q] = rows[m]
        inb[0, my_slot, q] = outb[0, self_dest, q]
        inb[1, my_slot, q] = outb[1, self_dest, q]

        for r in ([q - 1] if q < pairs - 1 else [q - 1, q]) if q else []:

            @pl.loop(1, dests)
            def _(k):
                send_rows(0, k, r)

    for q in range(pairs):
        last = q == pairs - 1
        for piece in range(PIECES):
            for way in range(2):
                if piece in pieces_of(way, last):
                    source = line - 1 if last else 2 * q + way
                    held = tok.at[source, pl.ds(piece * piece_rows, piece_rows)]
                    pltpu.make_async_copy(held, held, tok_r.at[source, piece]).wait()
                    if not last and piece in pieces_of(way, q + 2 == pairs):
                        start_hop(q + 2, way, piece)
        for source in range(2 * q, 2 * q + 2):
            if source != own:
                pltpu.make_async_copy(ids_ref, idb.at[source], ids_r.at[source]).wait()
        pick_rows(q)

    @pl.loop(1, dests)
    def _(k):
        d = (self_dest + k) % dests
        peer = (base2 + (d // 2) * stride2 + d % 2, xpos)
        pltpu.make_async_remote_copy(
            cnt_out.at[d], cnt_in.at[my_slot], cnt_s, cnt_r,
            device_id=peer, device_id_type=MESH,
        ).start()

    @pl.loop(1, dests)
    def _(k):
        send_rows(1, k, pl.ds(0, pairs))

    cnt_in[my_slot] = cnt_out[self_dest]

    def wait_rows(group, sem):
        view = inb.at[1 if group else 0, pl.ds(0, dests - 1), :, :, cut(group)]
        pltpu.make_async_copy(view, view, sem.at[group]).wait()

    def part(group, counts=True):
        first, size = ((0, body), (0, body_main), (body_main, body - body_main))[group]
        return pl.ds(first, size + (16 if counts and group == 2 else 0))

    def gram(group):
        wait_rows(group, row_r)
        i = 1 if group else 0
        wide = main if group == 1 else columns
        rows = inb[i, :, :, :, pl.ds(0, wide)].reshape(-1, wide)
        first = blocks - 1 if group == 2 else 0
        for b in range(first, blocks - 1 if group == 1 else blocks):
            start, stop = (0, columns) if b == blocks - 1 else (b * PANEL, main)
            product = lax.dot_general(
                rows[:, b * PANEL : (b + 1) * PANEL], rows[:, start:stop],
                (((0,), (0,)), ((), ())), preferred_element_type=F32,
            ).astype(BF16)
            for c in range(start // PANEL, stop // PANEL):
                t = tiles.index((b, c))
                for p in range(n_dp):
                    gram_out[i, p, t * part_rows : (t + 1) * part_rows, :] = product[
                        p * part_rows : (p + 1) * part_rows,
                        c * PANEL - start : (c + 1) * PANEL - start,
                    ]
        if group == 2:
            view = cnt_in.at[pl.ds(0, dests - 1)]
            pltpu.make_async_copy(view, view, cnt_r).wait()
            count = jnp.sum(cnt_in[...], axis=0)
            count = jnp.concatenate([count, jnp.zeros_like(count)], axis=0).astype(BF16)
            for p in range(n_dp):
                gram_out[i, p, body:, :] = count
        for d in range(1, n_dp):
            other = (xpos + d) % n_dp
            pltpu.make_async_remote_copy(
                gram_out.at[i, other, part(group)], gram_in.at[i, d - 1, part(group)],
                rs_s.at[group, d - 1], rs_r.at[group, d - 1],
                device_id=(idx, other), device_id_type=MESH,
            ).start()

    def wait_shares(group, sem):
        for d in range(1, n_dp):
            view = gram_in.at[1 if group else 0, d - 1, part(group)]
            pltpu.make_async_copy(view, view, sem.at[group, d - 1]).wait()

    def share(group):
        wait_shares(group, rs_r)
        i = 1 if group else 0
        total = gram_out[i, xpos, part(group)].astype(F32)
        for d in range(1, n_dp):
            total = total + gram_in[i, d - 1, part(group)].astype(F32)
        mine = part(group, False)
        whole[i, xpos, mine] = total[: mine.size].astype(BF16)
        for d in range(1, n_dp):
            other = (xpos + d) % n_dp
            pltpu.make_async_remote_copy(
                whole.at[i, xpos, mine], whole.at[i, xpos, mine],
                ag_s.at[group, d - 1], ag_r.at[group, d - 1],
                device_id=(idx, other), device_id_type=MESH,
            ).start()
        if group == 2:
            for expert in range(2):
                row = total[mine.size + expert : mine.size + expert + 1]
                total_cnt[expert] = jnp.broadcast_to(row, (8, PANEL))

    def wait_whole(group, sem):
        for d in range(1, n_dp):
            view = whole.at[1 if group else 0, (xpos + n_dp - d) % n_dp, part(group, False)]
            pltpu.make_async_copy(view, view, sem.at[group, d - 1]).wait()

    for load in loads:
        load.wait()
    weights(0)
    weights(1)
    gram(0)
    share(0)

    @pl.loop(1, dests)
    def _(k):
        send_rows(2, k, pl.ds(0, pairs))

    gram(1)
    gram(2)
    share(1)
    share(2)
    for group in range(3):
        wait_whole(group, ag_r)

    for group in range(3):
        wait_rows(group, row_s)
        wait_shares(group, rs_s)
        wait_whole(group, ag_s)
    view = cnt_in.at[pl.ds(0, dests - 1)]
    pltpu.make_async_copy(view, view, cnt_s).wait()
    for copy in hops:
        copy.wait_send()
    view = idb.at[pl.ds(0, line - 1)]
    pltpu.make_async_copy(view, view, ids_s).wait()


def last_kernel(n_dp, w_ref, change, whole, cnt, q_ref, ww_ref, hg_ref, hess):
    columns = w_ref.shape[2]
    blocks = columns // PANEL
    part_rows = PANEL // n_dp
    weights = w_ref[0].astype(F32) + change[0].astype(F32)
    q_ref[0] = weights[:, :PANEL].astype(BF16)
    ww_ref[0] = weights[:, PANEL:].astype(BF16)
    inverse = 1.0 / jnp.sum(cnt[0, :1], axis=1, keepdims=True)
    main = columns - PANEL
    for t, (b, c) in enumerate(tiles_of(blocks)):
        for p in range(n_dp):
            hess[b * PANEL + p * part_rows : b * PANEL + (p + 1) * part_rows,
                 c * PANEL : (c + 1) * PANEL] = whole[0, p, t * part_rows : (t + 1) * part_rows, :]
    def across(left, right):
        return lax.dot_general(left, right, (((1,), (1,)), ((), ())), preferred_element_type=F32)

    for c in range(blocks - 1):
        low, high = c * PANEL, (c + 1) * PANEL
        out = jnp.dot(change[0, :, :high], hess[:high, low:high], preferred_element_type=F32)
        out = out + jnp.dot(change[0, :, main:], hess[main:, low:high], preferred_element_type=F32)
        if high < main:
            out = out + across(change[0, :, high:main], hess[low:high, high:main])
        hg_ref[0, :, low:high] = out * inverse
    hg_ref[0, :, main:] = across(change[0], hess[main:]) * inverse


def per_device(tokens, expert_ids, weight_cols, uinv_panel, u_window, panel_index):
    n_expert, n_dp = lax.axis_size("expert"), lax.axis_size("dp")
    line = math.isqrt(n_expert // 2)
    dests = 2 * line
    rows, columns = weight_cols.shape[1:]
    n_tok, top_k = expert_ids.shape
    window = lax.dynamic_slice_in_dim(tokens, panel_index[0] * PANEL, columns, 1)
    blocks = columns // PANEL
    body = blocks * (blocks + 1) // 2 * (PANEL // n_dp)
    dma = pltpu.SemaphoreType.DMA
    vmem = pl.BlockSpec(memory_space=pltpu.VMEM)
    hbm = pl.BlockSpec(memory_space=pl.ANY)
    change, whole, cnt = pl.pallas_call(
        functools.partial(route_kernel, line, n_dp),
        out_shape=(
            jax.ShapeDtypeStruct((2, rows, columns), BF16),
            jax.ShapeDtypeStruct((2, n_dp, body, PANEL), BF16),
            jax.ShapeDtypeStruct((2, 8, PANEL), F32),
        ),
        in_specs=[vmem, vmem, hbm, hbm, hbm],
        out_specs=(vmem,) * 3,
        scratch_shapes=[
            pltpu.VMEM(weight_cols.shape, BF16),
            pltpu.VMEM(uinv_panel.shape, F32),
            pltpu.VMEM(u_window.shape, F32),
            pltpu.VMEM((line, n_tok, columns), BF16),
            pltpu.VMEM((line, top_k, n_tok), jnp.int32),
            pltpu.VMEM((2, dests, line // 2, 2 * SLOTS, columns), BF16),
            pltpu.VMEM((2, dests, line // 2, 2 * SLOTS, columns), BF16),
            pltpu.VMEM((dests, 8, n_tok), F32),
            pltpu.VMEM((dests, 8, n_tok), F32),
            pltpu.VMEM((2, n_dp, body + 16, PANEL), BF16),
            pltpu.VMEM((2, n_dp - 1, body + 16, PANEL), BF16),
            dma((3,)),
            dma((line, PIECES)), dma((line, PIECES)), dma, dma((line,)), dma((3,)), dma((3,)), dma, dma,
            dma((3, n_dp - 1)), dma((3, n_dp - 1)), dma((3, n_dp - 1)), dma((3, n_dp - 1)),
        ],
        compiler_params=pltpu.CompilerParams(
            collective_id=0, has_side_effects=True, vmem_limit_bytes=56 * 1024 * 1024
        ),
    )(window, expert_ids.T, weight_cols, uinv_panel, u_window)

    def per_expert(*shape):
        return pl.BlockSpec((1,) + shape, lambda i: (i,) + (0,) * len(shape))

    return pl.pallas_call(
        functools.partial(last_kernel, n_dp),
        grid=(2,),
        out_shape=(
            jax.ShapeDtypeStruct((2, rows, PANEL), BF16),
            jax.ShapeDtypeStruct((2, rows, columns - PANEL), BF16),
            jax.ShapeDtypeStruct((2, rows, columns), F32),
        ),
        in_specs=[
            per_expert(rows, columns), per_expert(rows, columns),
            per_expert(n_dp, body, PANEL), per_expert(8, PANEL),
        ],
        out_specs=(per_expert(rows, PANEL), per_expert(rows, columns - PANEL), per_expert(rows, columns)),
        scratch_shapes=[pltpu.VMEM((columns, columns), BF16)],
        compiler_params=pltpu.CompilerParams(vmem_limit_bytes=56 * 1024 * 1024),
    )(weight_cols, change, whole, cnt)


def solution(mesh):
    placed = (
        P(("expert", "dp"), None),
        P(("expert", "dp"), None),
        P("expert", "dp", None),
        P("expert", None, None),
        P("expert", None, None),
        P(),
    )
    return jax.shard_map(
        per_device,
        mesh=mesh,
        in_specs=placed,
        out_specs=(P("expert", "dp", None), P("expert", "dp", None), P("expert", "dp", None)),
        check_vma=False,
    )
```
